32 devices in a mesh: groups: 2 (over x), dtp: 16 (over z, y, core).
Axes of the slice: x: 2, y: 2, z: 4, core: 2. Of those that a mesh axis runs over, the one named last changes fastest.
Arguments:
- grad_dec: bfloat16 [64, 8192], P(('groups', 'dtp')), parts along dimension 0, may hold values from -6 to 6
- token_order: int32 [64], P('groups'), parts along dimension 0, may hold values from 0 to 31, each once
- proj_pre_codes: bfloat16 [64, 8192], P('groups', 'dtp'), parts along dimension 0, may hold values from -4 to 4
- proj_pre_exps: int32 [64, 64], P('groups', 'dtp'), parts along dimension 0, may hold values from 6 to 10
- projector_norm_input_codes: bfloat16 [64, 12800], P(('groups', 'dtp')), parts along dimension 0, may hold values from -4 to 4
- projector_norm_input_exponents: int32 [64, 100], P(('groups', 'dtp')), parts along dimension 0, may hold values from 6 to 10
- projector_norm_gain: float32 [12800], replicated, may hold values from 0.1 to 1.9
- projector_norm_bias: float32 [12800], replicated, may hold values from -3 to 3
- proj_weight: bfloat16 [12800, 8192], P(None, 'dtp'), may hold values from -0.0546875 to 0.0546875
- vit_pre_codes: bfloat16 [256, 12800], P('groups', 'dtp'), parts along dimension 0, may hold values from -4 to 4
- vit_pre_exps: int32 [2, 12800], P('groups', 'dtp'), parts along dimension 0, may hold values from 6 to 10
- vit_down: bfloat16 [12800, 3200], P('dtp'), may hold values from -0.0546875 to 0.0546875
- vit_up: bfloat16 [3200, 12800], P(None, 'dtp'), may hold values from -0.109375 to 0.109375
- vit_mid_codes: bfloat16 [256, 3200], P(('groups', 'dtp')), parts along dimension 0, may hold values from -4 to 4
- vit_mid_exps: int32 [256, 25], P(('groups', 'dtp')), parts along dimension 0, may hold values from 6 to 10
- mid_gain: float32 [3200], replicated, may hold values from 0.1 to 1.9
- layer_scale: float32 [3200], replicated, may hold values from 0.25 to 1
Outputs:
- grad_proj_weight: bfloat16 [12800, 16384], P(None, ('groups', 'dtp')), parts along dimension 1
- grad_vit_down: bfloat16 [12800, 6400], P('dtp', 'groups'), parts along dimension 1
- grad_vit_up: bfloat16 [3200, 25600], P(None, ('groups', 'dtp')), parts along dimension 1
- grad_vit_in: bfloat16 [256, 3200], P(('groups', 'dtp')), parts along dimension 0
The draws below stay inside these ranges and needn't reach their ends.
There are 2 independent parts, one for each index of `groups`. The reference program is written for one: setup_inputs(seed, part) draws one part's arguments, and reference() takes and returns one part's arrays. A program takes and returns all parts, laid end to end along the dimension named above; an argument that names none is the same for every part. Nothing has to cross between parts.
Inputs may be any that keep to these rules, and one draw needn't show every extreme that they name: A permutation: decoder position p holds encoder token token_order[p].
All inputs are finite; a program needn't handle non-finite values.
Results may differ from the reference program's by a relative error of at most 0.0075.
Values may be sent and summed in bfloat16 or wider, within the bound.
A program may use at most 128 MiB of HBM per device.

```python
import math
import jax
import jax.numpy as jnp
from jax import lax

D_VIT = 3200
FF_VIT = 12800
D_LLM = 8192
BLOCK = 128
D_PS = 12800
TOKENS = 32
VIT_TOKENS = 128


def set_ends(result, stream_key, least, largest):
    place = [jax.random.randint(jax.random.fold_in(stream_key, axis), (), 0, length) for axis, length in enumerate(result.shape)]
    widest = result.shape.index(max(result.shape))
    neighbour = place[:widest] + [(place[widest] + 1) % result.shape[widest]] + place[widest + 1:]
    return result.at[tuple(place)].set(least).at[tuple(neighbour)].set(largest)


def shard_levels(rng, extent, shards, low, top_value):
    factor_of = 1.0
    for axis_at, shards_of in shards:
        draws = jax.random.uniform(jax.random.fold_in(jax.random.fold_in(rng, 6), axis_at), (shards_of,), jnp.float32, low / len(shards), top_value / len(shards))
        factor_of = factor_of * jnp.repeat(jnp.exp(draws), extent[axis_at] // shards_of).reshape((-1,) + (1,) * (len(extent) - 1 - axis_at))
    return factor_of


def scatter_about(stream_key, extent, width, bound, pieces=(), held_as=jnp.bfloat16):
    result = jax.random.normal(stream_key, extent, jnp.float32) * width
    if len(pieces) > 0:
        result = shard_levels(stream_key, extent, pieces, -0.22, 0.18) * result
    return jnp.clip(result, min=-bound, max=bound).astype(held_as)


def setup_inputs(seed: int = 0, part: int = 0) -> dict:
    key_of = jax.random.split(jax.random.key(seed), 18)
    part_splits = jax.random.split(jax.random.fold_in(key_of[17], part), 18)
    return {
        "grad_dec": scatter_about(part_splits[0], (TOKENS, D_LLM), 1.0, 6.0, ((0, 16),)),
        "token_order": jax.random.permutation(part_splits[1], TOKENS).astype(jnp.int32),
        "proj_pre_codes": scatter_about(part_splits[2], (TOKENS, D_LLM), 1.0, 4.0, ((1, 16),)),
        "proj_pre_exps": set_ends(jax.random.randint(part_splits[3], (TOKENS, D_LLM // BLOCK), 6, 11), jax.random.fold_in(part_splits[3], 1), 6, 10).astype(jnp.int32),
        "projector_norm_input_codes": scatter_about(part_splits[4], (TOKENS, D_PS), 1.0, 4.0, ((0, 16),)),
        "projector_norm_input_exponents": set_ends(jax.random.randint(part_splits[5], (TOKENS, D_PS // BLOCK), 6, 11), jax.random.fold_in(part_splits[5], 1), 6, 10).astype(jnp.int32),
        "projector_norm_gain": jnp.clip(1.0 + 0.18 * jax.random.normal(key_of[6], (D_PS,), jnp.float32), 0.1, 1.9),
        "projector_norm_bias": scatter_about(key_of[7], (D_PS,), 0.5, 3.0, (), jnp.float32),
        "proj_weight": scatter_about(key_of[8], (D_PS, D_LLM), D_PS ** -0.5, 0.0546875, ((1, 16),)),
        "vit_pre_codes": scatter_about(part_splits[9], (VIT_TOKENS, FF_VIT), 1.0, 4.0, ((1, 16),)),
        "vit_pre_exps": set_ends(jax.random.randint(part_splits[10], (VIT_TOKENS // BLOCK, FF_VIT), 6, 11), jax.random.fold_in(part_splits[10], 1), 6, 10).astype(jnp.int32),
        "vit_down": scatter_about(key_of[11], (FF_VIT, D_VIT), FF_VIT ** -0.5, 0.0546875, ((0, 16),)),
        "vit_up": scatter_about(key_of[12], (D_VIT, FF_VIT), D_VIT ** -0.5, 0.109375, ((1, 16),)),
        "vit_mid_codes": scatter_about(part_splits[13], (VIT_TOKENS, D_VIT), 1.0, 4.0, ((0, 16),)),
        "vit_mid_exps": set_ends(jax.random.randint(part_splits[14], (VIT_TOKENS, D_VIT // BLOCK), 6, 11), jax.random.fold_in(part_splits[14], 1), 6, 10).astype(jnp.int32),
        "mid_gain": jnp.clip(1.0 + 0.18 * jax.random.normal(key_of[15], (D_VIT,), jnp.float32), 0.1, 1.9),
        "layer_scale": jnp.clip(jnp.exp(jax.random.uniform(key_of[16], (D_VIT,), jnp.float32, math.log(0.25), math.log(1.0))), 0.25, 1.0),
    }


def decode_block_columns(codes, exps):
    rows, cols = codes.shape
    groups = exps.shape[1]
    scale = jnp.exp2((exps - 8).astype(jnp.float32))
    return (codes.astype(jnp.float32).reshape(rows, groups, cols // groups) * scale[:, :, None]).reshape(rows, cols)

def dequant_rows(codes, exps):
    rows, cols = codes.shape
    groups = exps.shape[0]
    scale = jnp.exp2((exps - 8).astype(jnp.float32))
    return (codes.astype(jnp.float32).reshape(groups, rows // groups, cols) * scale[:, None, :]).reshape(rows, cols)

def gelu_grad(value):
    return 0.5 * (1.0 + jax.scipy.special.erf(value / math.sqrt(2.0))) + value * jnp.exp(-0.5 * value * value) / math.sqrt(2.0 * math.pi)

def layer_norm_statistics(merged):
    center = merged - lax.optimization_barrier(jnp.mean(merged, axis=-1, keepdims=True))
    inverse_deviation = lax.rsqrt(lax.optimization_barrier(jnp.mean(center * center, axis=-1, keepdims=True)) + 1e-05)
    return (center * inverse_deviation, inverse_deviation)

def layer_norm_backward(gradient_input, centered_unit_input, inverse_deviation, norm_gain_vector):
    gain_scaled_gradient = gradient_input * norm_gain_vector
    leading_moment = lax.optimization_barrier(jnp.mean(gain_scaled_gradient, axis=-1, keepdims=True))
    trailing_moment = lax.optimization_barrier(jnp.mean(gain_scaled_gradient * centered_unit_input, axis=-1, keepdims=True))
    return inverse_deviation * (gain_scaled_gradient - leading_moment - centered_unit_input * trailing_moment)

def rms_stats(mid):
    recip = lax.rsqrt(lax.optimization_barrier(jnp.mean(mid * mid, axis=-1, keepdims=True)) + 1e-06)
    return (mid * recip, recip)

def rms_back(gradient_input, uhat, recip, norm_gain_vector):
    gain_scaled_gradient = gradient_input * norm_gain_vector
    return recip * (gain_scaled_gradient - uhat * lax.optimization_barrier(jnp.mean(gain_scaled_gradient * uhat, axis=-1, keepdims=True)))

def reference(grad_dec, token_order, proj_pre_codes, proj_pre_exps, projector_norm_input_codes, projector_norm_input_exponents, projector_norm_gain, projector_norm_bias, proj_weight, vit_pre_codes, vit_pre_exps, vit_down, vit_up, vit_mid_codes, vit_mid_exps, mid_gain, layer_scale):
    f32 = jnp.float32
    brain_float_half = jnp.bfloat16
    grad_act = jnp.zeros_like(grad_dec).at[token_order].set(grad_dec)
    proj_pre = decode_block_columns(proj_pre_codes, proj_pre_exps)
    grad_pre = (grad_act.astype(f32) * gelu_grad(proj_pre)).astype(brain_float_half)
    centered_unit_input, inverse_deviation = layer_norm_statistics(decode_block_columns(projector_norm_input_codes, projector_norm_input_exponents))
    normalized_rows = (centered_unit_input * projector_norm_gain + projector_norm_bias).astype(brain_float_half)
    grad_proj_weight = lax.dot_general(normalized_rows, grad_pre, (((0,), (0,)), ((), ())), preferred_element_type=f32).astype(brain_float_half)
    normalized_gradient = lax.dot_general(grad_pre, proj_weight, (((1,), (1,)), ((), ())), preferred_element_type=f32)
    merged_token_gradient = layer_norm_backward(normalized_gradient, centered_unit_input, inverse_deviation, projector_norm_gain).astype(brain_float_half)
    grad_out = merged_token_gradient.reshape(VIT_TOKENS, D_VIT)
    pre = dequant_rows(vit_pre_codes, vit_pre_exps)
    hidden = jax.nn.gelu(pre, approximate=False).astype(brain_float_half)
    grad_branch = (grad_out.astype(f32) * layer_scale).astype(brain_float_half)
    grad_vit_down = lax.dot_general(hidden, grad_branch, (((0,), (0,)), ((), ())), preferred_element_type=f32).astype(brain_float_half)
    grad_hidden = lax.dot_general(grad_branch, vit_down, (((1,), (1,)), ((), ())), preferred_element_type=f32)
    grad_vit_pre = (grad_hidden * gelu_grad(pre)).astype(brain_float_half)
    uhat, recip = rms_stats(decode_block_columns(vit_mid_codes, vit_mid_exps))
    mid_normed = (uhat * mid_gain).astype(brain_float_half)
    grad_vit_up = lax.dot_general(mid_normed, grad_vit_pre, (((0,), (0,)), ((), ())), preferred_element_type=f32).astype(brain_float_half)
    grad_mid_normed = lax.dot_general(grad_vit_pre, vit_up, (((1,), (1,)), ((), ())), preferred_element_type=f32)
    grad_vit_in = (grad_out.astype(f32) + rms_back(grad_mid_normed, uhat, recip, mid_gain)).astype(brain_float_half)
    return (grad_proj_weight, grad_vit_down, grad_vit_up, grad_vit_in)
```

```python
import math

import jax
import jax.numpy as jnp
from jax import lax
from jax.experimental import pallas as pl
from jax.experimental.pallas import tpu as pltpu
from jax.sharding import PartitionSpec as P


def decode_block_columns(codes, exps):
    rows, cols = codes.shape
    groups = exps.shape[1]
    scale = jnp.exp2((exps - 8).astype(jnp.float32))
    return (
        codes.astype(jnp.float32).reshape(rows, groups, cols // groups) * scale[:, :, None]
    ).reshape(rows, cols)


def dequant_rows(codes, exps):
    rows, cols = codes.shape
    groups = exps.shape[0]
    scale = jnp.exp2((exps - 8).astype(jnp.float32))
    return (
        codes.astype(jnp.float32).reshape(groups, rows // groups, cols) * scale[:, None, :]
    ).reshape(rows, cols)


def gelu_grad(value):
    return 0.5 * (1.0 + jax.scipy.special.erf(value / math.sqrt(2.0))) + value * jnp.exp(
        -0.5 * value * value
    ) / math.sqrt(2.0 * math.pi)


def layer_norm_statistics(merged):
    center = merged - jnp.mean(merged, axis=-1, keepdims=True)
    inverse_deviation = lax.rsqrt(jnp.mean(center * center, axis=-1, keepdims=True) + 1e-05)
    return (center * inverse_deviation, inverse_deviation)


def layer_norm_backward(gradient_input, centered_unit_input, inverse_deviation, norm_gain_vector):
    gain_scaled_gradient = gradient_input * norm_gain_vector
    leading_moment = jnp.mean(gain_scaled_gradient, axis=-1, keepdims=True)
    trailing_moment = jnp.mean(gain_scaled_gradient * centered_unit_input, axis=-1, keepdims=True)
    return inverse_deviation * (
        gain_scaled_gradient - leading_moment - centered_unit_input * trailing_moment
    )


def rms_stats(mid):
    recip = lax.rsqrt(jnp.mean(mid * mid, axis=-1, keepdims=True) + 1e-06)
    return (mid * recip, recip)


def rms_back(gradient_input, uhat, recip, norm_gain_vector):
    gain_scaled_gradient = gradient_input * norm_gain_vector
    return recip * (
        gain_scaled_gradient - uhat * jnp.mean(gain_scaled_gradient * uhat, axis=-1, keepdims=True)
    )


def contract_rows(left, right):
    return lax.dot_general(
        left, right, (((0,), (0,)), ((), ())), preferred_element_type=jnp.float32
    )


def contract_cols(left, right):
    return lax.dot_general(
        left, right, (((1,), (1,)), ((), ())), preferred_element_type=jnp.float32
    )


def body(
    grad_dec,
    token_order,
    proj_pre_codes,
    proj_pre_exps,
    projector_norm_input_codes,
    projector_norm_input_exponents,
    projector_norm_gain,
    projector_norm_bias,
    proj_weight,
    vit_pre_codes,
    vit_pre_exps,
    vit_down,
    vit_up,
    vit_mid_codes,
    vit_mid_exps,
    mid_gain,
    layer_scale,
):
    f32 = jnp.float32
    brain_float_half = jnp.bfloat16
    own_vit = vit_mid_codes.shape[0]
    d_vit = vit_mid_codes.shape[1]
    uhat, recip = rms_stats(decode_block_columns(vit_mid_codes, vit_mid_exps))
    mid_normed = (uhat * mid_gain).astype(brain_float_half)
    received = lax.all_to_all(grad_dec, "dtp", split_axis=1, concat_axis=0, tiled=True)
    inverse = jnp.argsort(token_order)
    grad_act = jnp.take(received, inverse, axis=0)
    proj_pre = decode_block_columns(proj_pre_codes, proj_pre_exps)
    grad_pre = (grad_act.astype(f32) * gelu_grad(proj_pre)).astype(brain_float_half)
    pre = dequant_rows(vit_pre_codes, vit_pre_exps)
    hidden = jax.nn.gelu(pre, approximate=False).astype(brain_float_half)
    vit_rows_all = hidden.shape[0]
    merged_token_codes, merged_token_exponents = (
        lax.all_gather(projector_norm_input_codes, "dtp", axis=0, tiled=True),
        lax.all_gather(projector_norm_input_exponents, "dtp", axis=0, tiled=True),
    )
    centered_unit_input, inverse_deviation = layer_norm_statistics(
        decode_block_columns(merged_token_codes, merged_token_exponents)
    )
    normalized_rows = (centered_unit_input * projector_norm_gain + projector_norm_bias).astype(
        brain_float_half
    )
    grad_proj_weight = contract_rows(normalized_rows, grad_pre).astype(brain_float_half)
    normalized_gradient = contract_cols(grad_pre, proj_weight)
    merged_gradient_term = layer_norm_backward(
        normalized_gradient, centered_unit_input, inverse_deviation, projector_norm_gain
    )
    merged_token_gradient = lax.psum(merged_gradient_term, "dtp").astype(brain_float_half)
    grad_out_all = merged_token_gradient.reshape(vit_rows_all, d_vit)
    grad_out = lax.dynamic_slice_in_dim(grad_out_all, lax.axis_index("dtp") * own_vit, own_vit, 0)
    branch = (grad_out_all.astype(f32) * layer_scale).astype(brain_float_half)
    down_total = contract_rows(hidden, branch)
    grad_hidden = contract_cols(branch, vit_down)
    down_total, grad_hidden = (down_total, grad_hidden)
    grad_vit_down = down_total.astype(brain_float_half)
    grad_vit_pre = (grad_hidden * gelu_grad(pre)).astype(brain_float_half)
    rows = grad_vit_pre
    grad_vit_up = contract_rows(lax.all_gather(mid_normed, "dtp", axis=0, tiled=True), rows).astype(
        brain_float_half
    )
    rows = grad_vit_pre
    grad_mid_normed = lax.psum_scatter(
        contract_cols(rows, vit_up), "dtp", scatter_dimension=0, tiled=True
    )
    grad_vit_in = (grad_out.astype(f32) + rms_back(grad_mid_normed, uhat, recip, mid_gain)).astype(
        brain_float_half
    )
    return (grad_proj_weight, grad_vit_down, grad_vit_up, grad_vit_in)


FT = 640


def fused_kernel(
    gdec, tok, pp, mloc, gain, bias, pre_t, mid, mgain, lscale, w_h, vd_h, vu_h,
    gpw_h, gvd_h, gvu_h, gvin,
    wv, vdv, vuv, recv, mall, midall, goall, part, rc, ry, rz, sy, sz, acc, scr, nat,
    br, gp, gact, gvp_t, hid_t, gg_t, mu, rsd, stat, lsem, osem, ss, rsem,
):
    f32, b16 = jnp.float32, jnp.bfloat16
    d = lax.axis_index("dtp")
    z, y, c = d // 4, (d // 2) % 2, d % 2
    q_own = 2 * y + c
    core_peer, y_peer = d + 1 - 2 * c, d + 2 - 4 * y
    width = gp.shape[1]
    qw = nat.shape[1]
    tiles = qw // FT
    features = scr.shape[1]
    counter = [0]
    sent = []

    def sem_ids(n):
        counter[0] += n
        return counter[0] - n

    def copy(src, dst, i, peer):
        return pltpu.make_async_remote_copy(
            src_ref=src, dst_ref=dst, send_sem=ss.at[i], recv_sem=rsem.at[i],
            device_id={"dtp": peer}, device_id_type=pl.DeviceIdType.MESH,
        )

    def send(src, dst, i, peer):
        one = copy(src, dst, i, peer)
        one.start()
        sent.append(one)

    def lanes(t, base=0, size=FT):
        return pl.ds(pl.multiple_of(base + t * size, 128), size)

    order = [1 - c, 3 - c, 2 * (1 - y) + c, q_own]
    w_in = []
    for i, q in enumerate(order):
        rows = pl.ds(pl.multiple_of(q * qw, 128), qw)
        one = pltpu.make_async_copy(w_h.at[rows, :], wv.at[rows, :], lsem.at[i])
        one.start()
        w_in.append(one)
    vd_in = pltpu.make_async_copy(vd_h, vdv, lsem.at[4])
    vu_in = pltpu.make_async_copy(vu_h, vuv, lsem.at[5])
    vd_in.start()
    vu_in.start()

    barrier = pltpu.get_barrier_semaphore()
    for k in range(1, 16):
        pl.semaphore_signal(
            barrier, inc=1, device_id={"dtp": (d + k) % 16},
            device_id_type=pl.DeviceIdType.MESH,
        )
    pl.semaphore_wait(barrier, 15)

    class Gather:
        def __init__(self, buf):
            self.buf, self.base = buf, sem_ids(16)

        def go(self, owner, i, peer):
            send(self.buf.at[owner], self.buf.at[owner], self.base + i, peer)

        def arrive(self, owner, i):
            copy(self.buf.at[owner], self.buf.at[owner], self.base + i, core_peer).wait_recv()

        def start(self):
            for k in (1, 2, 3):
                self.go(d, k - 1, (z + k) % 4 * 4 + q_own)
            self.go(d, 3, y_peer)
            self.go(d, 7, core_peer)

        def forward_z(self):
            for k in (1, 3, 2):
                owner = (z + 4 - k) % 4 * 4 + q_own
                self.arrive(owner, k - 1)
                self.go(owner, 3 + k, y_peer)
                self.go(owner, 7 + k, core_peer)

        def forward_y(self):
            for k in (0, 1, 3, 2):
                owner = (z + 4 - k) % 4 * 4 + 2 * (1 - y) + c
                self.arrive(owner, 3 + k)
                self.go(owner, 11 + k, core_peer)

        def finish(self):
            for k in range(4):
                self.arrive((z + 4 - k) % 4 * 4 + 2 * y + 1 - c, 7 + k)
            for k in range(4):
                self.arrive((z + 4 - k) % 4 * 4 + 2 * (1 - y) + 1 - c, 11 + k)

    class Scatter:
        def __init__(self, r):
            self.r, self.base = r, sem_ids(6)

        def core(self, yy):
            send(part.at[self.r, 2 * yy + 1 - c], rc.at[self.r, yy], self.base + yy, core_peer)

        def core_wait(self, yy, i):
            copy(part.at[self.r, 2 * yy + 1 - c], rc.at[self.r, yy], self.base + i, core_peer).wait_recv()

        def middle(self):
            r = self.r

            @pl.loop(0, tiles)
            def _(t):
                s = lanes(t)
                sy[r, :, :, s] = (
                    part[r, 2 * (1 - y) + c, :, :, s].astype(f32)
                    + rc[r, 1 - y, :, :, s].astype(f32)
                ).astype(b16)

            send(sy.at[r], ry.at[r], self.base + 2, y_peer)

        def last(self):
            r = self.r
            copy(sy.at[r], ry.at[r], self.base + 2, y_peer).wait_recv()

            @pl.loop(0, tiles)
            def _(t):
                s = lanes(t)
                acc[:, :, s] = (
                    part[r, q_own, :, :, s].astype(f32) + rc[r, y, :, :, s].astype(f32)
                    + ry[r, :, :, s].astype(f32)
                )

            for k in (2, 1, 3):
                sz[r, k - 1] = acc[(z + k) % 4].astype(b16)
                send(sz.at[r, k - 1], rz.at[r, k - 1], self.base + 2 + k, (z + k) % 4 * 4 + q_own)

        def finish(self):
            r = self.r
            for k in (1, 2, 3):
                copy(sz.at[r, k - 1], rz.at[r, k - 1], self.base + 2 + k, core_peer).wait_recv()
            return (
                acc[z] + rz[r, 0].astype(f32) + rz[r, 1].astype(f32) + rz[r, 2].astype(f32)
            )

    a2a = sem_ids(16)

    def own_columns(p):
        return pl.ds(pl.multiple_of(p * width, 128), width)

    for k in range(1, 16):
        p = (d + k) % 16
        send(gdec.at[:, own_columns(p)], recv.at[d], a2a + k, p)
    mall[d] = mloc[...]
    g_in = Gather(mall)
    g_in.start()
    recv[d] = gdec[:, own_columns(d)]
    proj_grad = gelu_grad(pp[...].astype(f32))
    for k in range(1, 16):
        p = (d + 16 - k) % 16
        copy(recv.at[p], recv.at[p], a2a + k, p).wait_recv()
    for i in range(16):
        gact[2 * i : 2 * i + 2, :] = recv[i].astype(f32)
    place = (lax.broadcasted_iota(jnp.int32, (32, 32), 0) == tok[...]).astype(f32).astype(b16)
    grad_act = jnp.dot(place, gact[...].astype(b16), preferred_element_type=f32)
    gp[...] = (grad_act * proj_grad).astype(b16)

    s1 = Scatter(0)

    def project(i):
        q = order[i]
        w_in[i].wait()

        @pl.loop(0, tiles)
        def _(t):
            res = contract_cols(gp[...], wv[lanes(t, q * qw), :])
            part[0, q, :, :, lanes(t)] = res.reshape(4, 8, FT).astype(b16)

    project(0)
    s1.core(0)
    project(1)
    s1.core(1)
    g_in.forward_z()
    project(2)
    project(3)
    g_in.forward_y()
    s1.core_wait(0, 0)
    s1.core_wait(1, 1)
    s1.middle()

    def rms(t):
        s = lanes(t)
        v = mid[:, s].astype(f32)
        return jnp.sum(v * v, axis=-1, keepdims=True)

    rms_sum = lax.fori_loop(0, tiles, lambda t, a: a + rms(t), jnp.zeros((8, 1), f32))
    recip = lax.rsqrt(rms_sum / qw + 1e-06)

    @pl.loop(0, tiles)
    def _(t):
        s = lanes(t)
        midall[d, :, s] = (mid[:, s].astype(f32) * recip * mgain[:, s]).astype(b16)

    s1.last()
    g_mid = Gather(midall)
    g_mid.start()

    g_in.finish()
    all_tiles = features // FT
    zero = jnp.zeros((32, 1), f32)

    def mean_step(t, a):
        s = lanes(t)
        for i in range(16):
            scr[2 * i : 2 * i + 2, s] = mall[i, :, s].astype(f32)
        return a + jnp.sum(scr[:, s], axis=-1, keepdims=True)

    mean = lax.fori_loop(0, all_tiles, mean_step, zero) / features

    def var_step(t, a):
        s = lanes(t)
        center = scr[:, s] - mean
        scr[:, s] = center
        return a + jnp.sum(center * center, axis=-1, keepdims=True)

    variance = lax.fori_loop(0, all_tiles, var_step, zero) / features
    rsd[...] = jnp.broadcast_to(lax.rsqrt(variance + 1e-05), rsd.shape)

    total = s1.finish()
    own_rows = pl.ds(pl.multiple_of(z * 8, 8), 8)
    own_lanes = pl.ds(pl.multiple_of(q_own * qw, 128), qw)
    rstd8 = rsd[own_rows, 0:1]
    gy = total * gain[:, own_lanes]
    xh = scr[own_rows, own_lanes] * rstd8
    first = jnp.sum(gy, axis=-1, keepdims=True)
    second = jnp.sum(gy * xh, axis=-1, keepdims=True)
    lane = lax.broadcasted_iota(jnp.int32, (8, 128), 1)
    stat[0] = jnp.where(lane < 64, first, second)
    st = sem_ids(3)
    plane = [core_peer, y_peer, 4 * z + 3 - q_own]
    for j in range(3):
        send(stat.at[0], stat.at[j + 1], st + j, plane[j])
    for j in range(3):
        copy(stat.at[0], stat.at[j + 1], st + j, plane[j]).wait_recv()
    sums = (stat[0] + stat[1] + stat[2] + stat[3]) / features
    lead, trail = sums[:, 0:1], sums[:, 64:65]
    goall[d] = (rstd8 * (gy - lead - xh * trail)).astype(b16)
    g_out = Gather(goall)
    g_out.start()

    outs = []

    def weight_grad(h):
        @pl.loop(0, tiles)
        def _(t):
            s = lanes(t, h * qw)
            normed = (scr[:, s] * rsd[:, 0:1] * gain[:, s] + bias[:, s]).astype(b16)
            wv[s, :] = contract_rows(normed, gp[...]).astype(b16)

        rows = pl.ds(h * qw, qw)
        one = pltpu.make_async_copy(wv.at[rows, :], gpw_h.at[rows, :], osem.at[h])
        one.start()
        outs.append(one)

    weight_grad(0)
    g_out.forward_z()
    g_mid.forward_z()
    units = 160

    @pl.loop(0, vdv.shape[0] // units)
    def _(t):
        s = pl.ds(pl.multiple_of(t * units, 32), units)
        v = pre_t[s, :].astype(f32)
        cdf = 0.5 * (1.0 + lax.erf(v / math.sqrt(2.0)))
        hid_t[s, :] = (v * cdf).astype(b16)
        gg_t[s, :] = cdf + v * jnp.exp(-0.5 * v * v) / math.sqrt(2.0 * math.pi)

    g_out.forward_y()
    g_mid.forward_y()
    weight_grad(1)
    g_out.finish()

    vrow = lax.broadcasted_iota(jnp.int32, (128, 128), 0)
    held = lax.broadcasted_iota(jnp.int32, (128, 128), 1)
    vision = held // 32 * 32 + held % 8 * 4 + held // 8 % 4
    shuffle = (vrow == vision).astype(f32).astype(b16)

    @pl.loop(0, tiles)
    def _(t):
        s = lanes(t)
        block = goall[:, :, s].astype(f32).reshape(128, FT).astype(b16)
        rows = jnp.dot(shuffle, block, preferred_element_type=f32)
        nat[:, s] = rows
        br[:, s] = (rows * lscale[:, s]).astype(b16)

    vd_in.wait()

    @pl.loop(0, vdv.shape[0] // units)
    def _(t):
        s = pl.ds(pl.multiple_of(t * units, 32), units)
        gvp_t[s, :] = (contract_cols(vdv[s, :], br[...]) * gg_t[s, :]).astype(b16)

    vu_in.wait()

    @pl.loop(0, tiles)
    def _(t):
        s = lanes(t)
        res = contract_rows(gvp_t[...], vuv[:, s]).reshape(4, 4, 8, FT)
        for q in range(4):
            part[1, q, :, :, s] = res[:, q].astype(b16)

    s2 = Scatter(1)
    s2.core(0)
    s2.core(1)
    weight_grad(2)
    s2.core_wait(0, 0)
    s2.core_wait(1, 1)
    s2.middle()

    @pl.loop(0, vdv.shape[0] // units)
    def _(t):
        s = pl.ds(pl.multiple_of(t * units, 32), units)
        vdv[s, :] = jnp.dot(hid_t[s, :], br[...], preferred_element_type=f32).astype(b16)

    one = pltpu.make_async_copy(vdv, gvd_h, osem.at[4])
    one.start()
    outs.append(one)
    s2.last()
    g_mid.finish()

    @pl.loop(0, tiles)
    def _(t):
        s = lanes(t)
        block = midall[:, :, s].astype(f32).reshape(128, FT).astype(b16)
        vuv[:, s] = jnp.dot(gvp_t[...], block, preferred_element_type=f32).astype(b16)

    one = pltpu.make_async_copy(vuv, gvu_h, osem.at[5])
    one.start()
    outs.append(one)
    weight_grad(3)
    gn = s2.finish() * mgain[...]
    uhat = mid[...].astype(f32) * recip
    back = recip * (gn - uhat * jnp.mean(gn * uhat, axis=-1, keepdims=True))
    gvin[...] = (nat[pl.ds(pl.multiple_of(d * 8, 8), 8), :] + back).astype(b16)
    for one in sent:
        one.wait_send()
    for one in outs:
        one.wait()


def fused_body(
    grad_dec, token_order, proj_pre_codes, proj_pre_exps, projector_norm_input_codes,
    projector_norm_input_exponents, projector_norm_gain, projector_norm_bias, proj_weight,
    vit_pre_codes, vit_pre_exps, vit_down, vit_up, vit_mid_codes, vit_mid_exps, mid_gain,
    layer_scale,
):
    f32, b16 = jnp.float32, jnp.bfloat16
    merged = decode_block_columns(
        projector_norm_input_codes, projector_norm_input_exponents
    ).astype(b16)
    mid = decode_block_columns(vit_mid_codes, vit_mid_exps).astype(b16)
    pre_t = dequant_rows(vit_pre_codes, vit_pre_exps).astype(b16).T
    proj_pre = decode_block_columns(proj_pre_codes, proj_pre_exps).astype(b16)
    features, width = proj_weight.shape
    units, d_vit = vit_down.shape
    vmem = pl.BlockSpec(memory_space=pltpu.VMEM)
    hbm = pl.BlockSpec(memory_space=pl.ANY)
    scratch = [
        ((features, width), b16), ((units, d_vit), b16), ((units, d_vit), b16),
        ((16, 2, width), b16), ((16, 2, features), b16), ((16, 8, d_vit), b16),
        ((16, 8, d_vit), b16), ((2, 4, 4, 8, d_vit), b16), ((2, 2, 4, 8, d_vit), b16),
        ((2, 4, 8, d_vit), b16), ((2, 3, 8, d_vit), b16), ((2, 4, 8, d_vit), b16),
        ((2, 3, 8, d_vit), b16), ((4, 8, d_vit), f32), ((32, features), f32),
        ((128, d_vit), f32), ((128, d_vit), b16), ((32, width), b16), ((32, width), f32),
        ((units, 128), b16), ((units, 128), b16), ((units, 128), f32), ((32, 128), f32),
        ((32, 128), f32), ((4, 8, 128), f32),
    ]
    gpw, gvd, gvu, gvin = pl.pallas_call(
        fused_kernel,
        out_shape=(
            jax.ShapeDtypeStruct((features, width), b16),
            jax.ShapeDtypeStruct((units, d_vit), b16),
            jax.ShapeDtypeStruct((units, d_vit), b16),
            jax.ShapeDtypeStruct((8, d_vit), b16),
        ),
        in_specs=[vmem] * 10 + [hbm] * 3,
        out_specs=(hbm, hbm, hbm, vmem),
        scratch_shapes=[pltpu.VMEM(s, t) for s, t in scratch]
        + [
            pltpu.SemaphoreType.DMA((6,)), pltpu.SemaphoreType.DMA((6,)),
            pltpu.SemaphoreType.DMA((80,)), pltpu.SemaphoreType.DMA((80,)),
        ],
        compiler_params=pltpu.CompilerParams(
            collective_id=0, has_side_effects=True, vmem_limit_bytes=60 * 2**20
        ),
        cost_estimate=pl.CostEstimate(
            flops=3 * 10**9, bytes_accessed=48 * 10**6, transcendentals=2 * 10**5
        ),
    )(
        grad_dec, token_order.reshape(1, -1), proj_pre, merged,
        projector_norm_gain.reshape(1, -1), projector_norm_bias.reshape(1, -1), pre_t, mid,
        mid_gain.reshape(1, -1), layer_scale.reshape(1, -1), proj_weight, vit_down, vit_up.T,
    )
    return gpw, gvd, gvu.T, gvin


def solution(mesh):
    fused = mesh.shape["dtp"] == 16
    return jax.shard_map(
        fused_body if fused else body,
        mesh=mesh,
        in_specs=(
            P(("groups", "dtp"), None),
            P("groups"),
            P("groups", "dtp"),
            P("groups", "dtp"),
            P(("groups", "dtp"), None),
            P(("groups", "dtp"), None),
            P(),
            P(),
            P(None, "dtp"),
            P("groups", "dtp"),
            P("groups", "dtp"),
            P("dtp", None),
            P(None, "dtp"),
            P(("groups", "dtp"), None),
            P(("groups", "dtp"), None),
            P(),
            P(),
        ),
        out_specs=(
            P(None, ("groups", "dtp")),
            P("dtp", "groups"),
            P(None, ("groups", "dtp")),
            P(("groups", "dtp"), None),
        ),
        check_vma=False,
    )
```

```python
import math

import jax
import jax.numpy as jnp
from jax import lax
from jax.experimental import pallas as pl
from jax.experimental.pallas import tpu as pltpu
from jax.sharding import PartitionSpec as P


def decode_block_columns(codes, exps):
    rows, cols = codes.shape
    groups = exps.shape[1]
    scale = jnp.exp2((exps - 8).astype(jnp.float32))
    return (
        codes.astype(jnp.float32).reshape(rows, groups, cols // groups) * scale[:, :, None]
    ).reshape(rows, cols)


def dequant_rows(codes, exps):
    rows, cols = codes.shape
    groups = exps.shape[0]
    scale = jnp.exp2((exps - 8).astype(jnp.float32))
    return (
        codes.astype(jnp.float32).reshape(groups, rows // groups, cols) * scale[:, None, :]
    ).reshape(rows, cols)


def gelu_grad(value):
    return 0.5 * (1.0 + jax.scipy.special.erf(value / math.sqrt(2.0))) + value * jnp.exp(
        -0.5 * value * value
    ) / math.sqrt(2.0 * math.pi)


def layer_norm_statistics(merged):
    center = merged - jnp.mean(merged, axis=-1, keepdims=True)
    inverse_deviation = lax.rsqrt(jnp.mean(center * center, axis=-1, keepdims=True) + 1e-05)
    return (center * inverse_deviation, inverse_deviation)


def layer_norm_backward(gradient_input, centered_unit_input, inverse_deviation, norm_gain_vector):
    gain_scaled_gradient = gradient_input * norm_gain_vector
    leading_moment = jnp.mean(gain_scaled_gradient, axis=-1, keepdims=True)
    trailing_moment = jnp.mean(gain_scaled_gradient * centered_unit_input, axis=-1, keepdims=True)
    return inverse_deviation * (
        gain_scaled_gradient - leading_moment - centered_unit_input * trailing_moment
    )


def rms_stats(mid):
    recip = lax.rsqrt(jnp.mean(mid * mid, axis=-1, keepdims=True) + 1e-06)
    return (mid * recip, recip)


def rms_back(gradient_input, uhat, recip, norm_gain_vector):
    gain_scaled_gradient = gradient_input * norm_gain_vector
    return recip * (
        gain_scaled_gradient - uhat * jnp.mean(gain_scaled_gradient * uhat, axis=-1, keepdims=True)
    )


def contract_rows(left, right):
    return lax.dot_general(
        left, right, (((0,), (0,)), ((), ())), preferred_element_type=jnp.float32
    )


def contract_cols(left, right):
    return lax.dot_general(
        left, right, (((1,), (1,)), ((), ())), preferred_element_type=jnp.float32
    )


def body(
    grad_dec,
    token_order,
    proj_pre_codes,
    proj_pre_exps,
    projector_norm_input_codes,
    projector_norm_input_exponents,
    projector_norm_gain,
    projector_norm_bias,
    proj_weight,
    vit_pre_codes,
    vit_pre_exps,
    vit_down,
    vit_up,
    vit_mid_codes,
    vit_mid_exps,
    mid_gain,
    layer_scale,
):
    f32 = jnp.float32
    brain_float_half = jnp.bfloat16
    own_vit = vit_mid_codes.shape[0]
    d_vit = vit_mid_codes.shape[1]
    uhat, recip = rms_stats(decode_block_columns(vit_mid_codes, vit_mid_exps))
    mid_normed = (uhat * mid_gain).astype(brain_float_half)
    received = lax.all_to_all(grad_dec, "dtp", split_axis=1, concat_axis=0, tiled=True)
    inverse = jnp.argsort(token_order)
    grad_act = jnp.take(received, inverse, axis=0)
    proj_pre = decode_block_columns(proj_pre_codes, proj_pre_exps)
    grad_pre = (grad_act.astype(f32) * gelu_grad(proj_pre)).astype(brain_float_half)
    pre = dequant_rows(vit_pre_codes, vit_pre_exps)
    hidden = jax.nn.gelu(pre, approximate=False).astype(brain_float_half)
    vit_rows_all = hidden.shape[0]
    merged_token_codes, merged_token_exponents = (
        lax.all_gather(projector_norm_input_codes, "dtp", axis=0, tiled=True),
        lax.all_gather(projector_norm_input_exponents, "dtp", axis=0, tiled=True),
    )
    centered_unit_input, inverse_deviation = layer_norm_statistics(
        decode_block_columns(merged_token_codes, merged_token_exponents)
    )
    normalized_rows = (centered_unit_input * projector_norm_gain + projector_norm_bias).astype(
        brain_float_half
    )
    grad_proj_weight = contract_rows(normalized_rows, grad_pre).astype(brain_float_half)
    normalized_gradient = contract_cols(grad_pre, proj_weight)
    merged_gradient_term = layer_norm_backward(
        normalized_gradient, centered_unit_input, inverse_deviation, projector_norm_gain
    )
    merged_token_gradient = lax.psum(merged_gradient_term, "dtp").astype(brain_float_half)
    grad_out_all = merged_token_gradient.reshape(vit_rows_all, d_vit)
    grad_out = lax.dynamic_slice_in_dim(grad_out_all, lax.axis_index("dtp") * own_vit, own_vit, 0)
    branch = (grad_out_all.astype(f32) * layer_scale).astype(brain_float_half)
    down_total = contract_rows(hidden, branch)
    grad_hidden = contract_cols(branch, vit_down)
    down_total, grad_hidden = (down_total, grad_hidden)
    grad_vit_down = down_total.astype(brain_float_half)
    grad_vit_pre = (grad_hidden * gelu_grad(pre)).astype(brain_float_half)
    rows = grad_vit_pre
    grad_vit_up = contract_rows(lax.all_gather(mid_normed, "dtp", axis=0, tiled=True), rows).astype(
        brain_float_half
    )
    rows = grad_vit_pre
    grad_mid_normed = lax.psum_scatter(
        contract_cols(rows, vit_up), "dtp", scatter_dimension=0, tiled=True
    )
    grad_vit_in = (grad_out.astype(f32) + rms_back(grad_mid_normed, uhat, recip, mid_gain)).astype(
        brain_float_half
    )
    return (grad_proj_weight, grad_vit_down, grad_vit_up, grad_vit_in)


FT = 640
BLOCK = 128


def fused_kernel(
    gdec, tok, ppc, ppe, mlc, mle, gain2, bias2, pre_c, pre_e, midc, mide, mgain2, lscale2,
    w_h, vd_h, vu_h,
    normed, gp, hid_t, br, gvp_t, midn, gvin,
    wv, vdv, vuv, recv, mall, midall, goall, part, rc, ry, rz, sy, sz, acc, scr, nat,
    gact, gg_t, pre_t, mid, gain, bias, mgain, lscale, rsd, stat, lsem, ss, rsem,
):
    f32, b16 = jnp.float32, jnp.bfloat16
    d = lax.axis_index("dtp")
    z, y, c = d // 4, (d // 2) % 2, d % 2
    q_own = 2 * y + c
    core_peer, y_peer = d + 1 - 2 * c, d + 2 - 4 * y
    width = gp.shape[1]
    qw = nat.shape[1]
    tiles = qw // FT
    features = scr.shape[1]
    counter = [0]
    sent = []

    def sem_ids(n):
        counter[0] += n
        return counter[0] - n

    def copy(src, dst, i, peer):
        return pltpu.make_async_remote_copy(
            src_ref=src, dst_ref=dst, send_sem=ss.at[i], recv_sem=rsem.at[i],
            device_id={"dtp": peer}, device_id_type=pl.DeviceIdType.MESH,
        )

    def send(src, dst, i, peer):
        one = copy(src, dst, i, peer)
        one.start()
        sent.append(one)

    def lanes(t, base=0, size=FT):
        return pl.ds(pl.multiple_of(base + t * size, 128), size)

    order = [1 - c, 3 - c, 2 * (1 - y) + c, q_own]
    w_in = []
    for i, q in enumerate(order):
        rows = pl.ds(pl.multiple_of(q * qw, 128), qw)
        one = pltpu.make_async_copy(w_h.at[rows, :], wv.at[rows, :], lsem.at[i])
        one.start()
        w_in.append(one)
    vd_in = pltpu.make_async_copy(vd_h, vdv, lsem.at[4])
    vu_in = pltpu.make_async_copy(vu_h, vuv, lsem.at[5])
    vd_in.start()
    vu_in.start()

    barrier = pltpu.get_barrier_semaphore()
    for k in range(1, 16):
        pl.semaphore_signal(
            barrier, inc=1, device_id={"dtp": (d + k) % 16},
            device_id_type=pl.DeviceIdType.MESH,
        )
    pl.semaphore_wait(barrier, 15)

    class Gather:
        def __init__(self, buf):
            self.buf, self.base = buf, sem_ids(16)

        def go(self, owner, i, peer):
            send(self.buf.at[owner], self.buf.at[owner], self.base + i, peer)

        def arrive(self, owner, i):
            copy(self.buf.at[owner], self.buf.at[owner], self.base + i, core_peer).wait_recv()

        def start(self):
            for k in (1, 2, 3):
                self.go(d, k - 1, (z + k) % 4 * 4 + q_own)
            self.go(d, 3, y_peer)
            self.go(d, 7, core_peer)

        def forward_z(self):
            for k in (1, 3, 2):
                owner = (z + 4 - k) % 4 * 4 + q_own
                self.arrive(owner, k - 1)
                self.go(owner, 3 + k, y_peer)
                self.go(owner, 7 + k, core_peer)

        def forward_y(self):
            for k in (0, 1, 3, 2):
                owner = (z + 4 - k) % 4 * 4 + 2 * (1 - y) + c
                self.arrive(owner, 3 + k)
                self.go(owner, 11 + k, core_peer)

        def finish(self):
            for k in range(4):
                self.arrive((z + 4 - k) % 4 * 4 + 2 * y + 1 - c, 7 + k)
            for k in range(4):
                self.arrive((z + 4 - k) % 4 * 4 + 2 * (1 - y) + 1 - c, 11 + k)

    class Scatter:
        def __init__(self, r):
            self.r, self.base = r, sem_ids(6)

        def core(self, yy):
            send(part.at[self.r, 2 * yy + 1 - c], rc.at[self.r, yy], self.base + yy, core_peer)

        def core_wait(self, yy, i):
            copy(part.at[self.r, 2 * yy + 1 - c], rc.at[self.r, yy], self.base + i, core_peer).wait_recv()

        def middle(self):
            r = self.r

            @pl.loop(0, tiles)
            def _(t):
                s = lanes(t)
                sy[r, :, :, s] = (
                    part[r, 2 * (1 - y) + c, :, :, s].astype(f32)
                    + rc[r, 1 - y, :, :, s].astype(f32)
                ).astype(b16)

            send(sy.at[r], ry.at[r], self.base + 2, y_peer)

        def last(self):
            r = self.r
            copy(sy.at[r], ry.at[r], self.base + 2, y_peer).wait_recv()

            @pl.loop(0, tiles)
            def _(t):
                s = lanes(t)
                acc[:, :, s] = (
                    part[r, q_own, :, :, s].astype(f32) + rc[r, y, :, :, s].astype(f32)
                    + ry[r, :, :, s].astype(f32)
                )

            for k in (2, 1, 3):
                sz[r, k - 1] = acc[(z + k) % 4].astype(b16)
                send(sz.at[r, k - 1], rz.at[r, k - 1], self.base + 2 + k, (z + k) % 4 * 4 + q_own)

        def finish(self):
            r = self.r
            for k in (1, 2, 3):
                copy(sz.at[r, k - 1], rz.at[r, k - 1], self.base + 2 + k, core_peer).wait_recv()
            return (
                acc[z] + rz[r, 0].astype(f32) + rz[r, 1].astype(f32) + rz[r, 2].astype(f32)
            )

    a2a = sem_ids(16)

    def own_columns(p):
        return pl.ds(pl.multiple_of(p * width, 128), width)

    for k in range(1, 16):
        p = (d + k) % 16
        send(gdec.at[:, own_columns(p)], recv.at[d], a2a + k, p)
    mscale = jnp.exp2((mle[...] - 8).astype(f32))
    for j in range(features // BLOCK):
        s = pl.ds(j * BLOCK, BLOCK)
        mall[d, :, s] = (mlc[:, s].astype(f32) * mscale[:, j : j + 1]).astype(b16)
    g_in = Gather(mall)
    g_in.start()
    recv[d] = gdec[:, own_columns(d)]
    pscale = jnp.exp2((ppe[...] - 8).astype(f32))
    proj_grad = jnp.concatenate(
        [
            gelu_grad(ppc[:, BLOCK * j : BLOCK * (j + 1)].astype(f32) * pscale[:, j : j + 1])
            for j in range(width // BLOCK)
        ],
        axis=1,
    )
    for k in range(1, 16):
        p = (d + 16 - k) % 16
        copy(recv.at[p], recv.at[p], a2a + k, p).wait_recv()
    for i in range(16):
        gact[2 * i : 2 * i + 2, :] = recv[i].astype(f32)
    place = (lax.broadcasted_iota(jnp.int32, (32, 32), 0) == tok[...]).astype(f32).astype(b16)
    grad_act = jnp.dot(place, gact[...].astype(b16), preferred_element_type=f32)
    gp[...] = (grad_act * proj_grad).astype(b16)

    s1 = Scatter(0)

    def project(i):
        q = order[i]
        w_in[i].wait()

        @pl.loop(0, tiles)
        def _(t):
            res = contract_cols(gp[...], wv[lanes(t, q * qw), :])
            part[0, q, :, :, lanes(t)] = res.reshape(4, 8, FT).astype(b16)

    project(0)
    s1.core(0)
    project(1)
    s1.core(1)
    g_in.forward_z()
    project(2)
    project(3)
    g_in.forward_y()
    s1.core_wait(0, 0)
    s1.core_wait(1, 1)
    s1.middle()

    for flat, line in ((gain2, gain), (bias2, bias), (mgain2, mgain), (lscale2, lscale)):
        for j in range(flat.shape[0]):
            line[:, BLOCK * j : BLOCK * (j + 1)] = flat[j : j + 1, :]
    dscale = jnp.exp2((mide[...] - 8).astype(f32))
    for j in range(qw // BLOCK):
        s = pl.ds(j * BLOCK, BLOCK)
        mid[:, s] = midc[:, s].astype(f32) * dscale[:, j : j + 1]

    def rms(t):
        s = lanes(t)
        v = mid[:, s]
        return jnp.sum(v * v, axis=-1, keepdims=True)

    rms_sum = lax.fori_loop(0, tiles, lambda t, a: a + rms(t), jnp.zeros((8, 1), f32))
    recip = lax.rsqrt(rms_sum / qw + 1e-06)

    @pl.loop(0, tiles)
    def _(t):
        s = lanes(t)
        midall[d, :, s] = (mid[:, s] * recip * mgain[:, s]).astype(b16)

    s1.last()
    g_mid = Gather(midall)
    g_mid.start()

    g_in.finish()
    all_tiles = features // FT
    zero = jnp.zeros((32, 1), f32)

    def mean_step(t, a):
        s = lanes(t)
        for i in range(16):
            scr[2 * i : 2 * i + 2, s] = mall[i, :, s].astype(f32)
        return a + jnp.sum(scr[:, s], axis=-1, keepdims=True)

    mean = lax.fori_loop(0, all_tiles, mean_step, zero) / features

    def var_step(t, a):
        s = lanes(t)
        center = scr[:, s] - mean
        scr[:, s] = center
        return a + jnp.sum(center * center, axis=-1, keepdims=True)

    variance = lax.fori_loop(0, all_tiles, var_step, zero) / features
    rsd[...] = jnp.broadcast_to(lax.rsqrt(variance + 1e-05), rsd.shape)

    total = s1.finish()
    own_rows = pl.ds(pl.multiple_of(z * 8, 8), 8)
    own_lanes = pl.ds(pl.multiple_of(q_own * qw, 128), qw)
    rstd8 = rsd[own_rows, 0:1]
    gy = total * gain[:, own_lanes]
    xh = scr[own_rows, own_lanes] * rstd8
    first = jnp.sum(gy, axis=-1, keepdims=True)
    second = jnp.sum(gy * xh, axis=-1, keepdims=True)
    lane = lax.broadcasted_iota(jnp.int32, (8, 128), 1)
    stat[0] = jnp.where(lane < 64, first, second)
    st = sem_ids(3)
    plane = [core_peer, y_peer, 4 * z + 3 - q_own]
    for j in range(3):
        send(stat.at[0], stat.at[j + 1], st + j, plane[j])
    for j in range(3):
        copy(stat.at[0], stat.at[j + 1], st + j, plane[j]).wait_recv()
    sums = (stat[0] + stat[1] + stat[2] + stat[3]) / features
    lead, trail = sums[:, 0:1], sums[:, 64:65]
    goall[d] = (rstd8 * (gy - lead - xh * trail)).astype(b16)
    g_out = Gather(goall)
    g_out.start()

    g_out.forward_z()
    spread = jnp.broadcast_to(jnp.exp2((pre_e[...] - 8).astype(f32)) / 16, (16, vdv.shape[0]))
    pre_t[...] = contract_rows(spread.astype(b16), jnp.ones((16, 128), b16))
    units = 160

    @pl.loop(0, vdv.shape[0] // units)
    def _(t):
        s = pl.ds(pl.multiple_of(t * units, 32), units)
        v = pre_c[s, :].astype(f32) * pre_t[s, :]
        cdf = 0.5 * (1.0 + lax.erf(v / math.sqrt(2.0)))
        hid_t[s, :] = (v * cdf).astype(b16)
        gg_t[s, :] = cdf + v * jnp.exp(-0.5 * v * v) / math.sqrt(2.0 * math.pi)

    g_out.forward_y()
    g_mid.forward_z()
    g_out.finish()

    vrow = lax.broadcasted_iota(jnp.int32, (128, 128), 0)
    held = lax.broadcasted_iota(jnp.int32, (128, 128), 1)
    vision = held // 32 * 32 + held % 8 * 4 + held // 8 % 4
    shuffle = (vrow == vision).astype(f32).astype(b16)

    @pl.loop(0, tiles)
    def _(t):
        s = lanes(t)
        block = goall[:, :, s].astype(f32).reshape(128, FT).astype(b16)
        rows = jnp.dot(shuffle, block, preferred_element_type=f32)
        nat[:, s] = rows
        br[:, s] = (rows * lscale[:, s]).astype(b16)

    vd_in.wait()

    @pl.loop(0, vdv.shape[0] // units)
    def _(t):
        s = pl.ds(pl.multiple_of(t * units, 32), units)
        gvp_t[s, :] = (contract_cols(vdv[s, :], br[...]) * gg_t[s, :]).astype(b16)

    vu_in.wait()

    @pl.loop(0, tiles)
    def _(t):
        s = lanes(t)
        res = contract_rows(gvp_t[...], vuv[:, s]).reshape(4, 4, 8, FT)
        for q in range(4):
            part[1, q, :, :, s] = res[:, q].astype(b16)

    s2 = Scatter(1)
    s2.core(0)
    s2.core(1)
    g_mid.forward_y()
    s2.core_wait(0, 0)
    s2.core_wait(1, 1)
    s2.middle()

    @pl.loop(0, features // FT)
    def _(t):
        s = lanes(t)
        normed[:, s] = (scr[:, s] * rsd[:, 0:1] * gain[:, s] + bias[:, s]).astype(b16)

    s2.last()
    g_mid.finish()

    @pl.loop(0, tiles)
    def _(t):
        s = lanes(t)
        midn[:, s] = midall[:, :, s].astype(f32).reshape(128, FT).astype(b16)

    gn = s2.finish() * mgain[...]
    uhat = mid[...] * recip
    back = recip * (gn - uhat * jnp.mean(gn * uhat, axis=-1, keepdims=True))
    gvin[...] = (nat[pl.ds(pl.multiple_of(d * 8, 8), 8), :] + back).astype(b16)
    for one in sent:
        one.wait_send()


def weights_kernel(normed, gp, hid_t, br, gvp_t, midn, gvin, gpw, gvd, gvu, out):
    f32, b16 = jnp.float32, jnp.bfloat16
    step = pl.program_id(0)
    gpw[...] = contract_rows(normed[...], gp[...]).astype(b16)

    @pl.when(step % 5 == 0)
    def _():
        gvd[...] = jnp.dot(hid_t[...], br[...], preferred_element_type=f32).astype(b16)

    @pl.when(step % 5 == 2)
    def _():
        gvu[...] = jnp.dot(gvp_t[...], midn[...], preferred_element_type=f32).astype(b16)

    @pl.when(step == 0)
    def _():
        out[...] = gvin[...]


def fused_body(
    grad_dec, token_order, proj_pre_codes, proj_pre_exps, projector_norm_input_codes,
    projector_norm_input_exponents, projector_norm_gain, projector_norm_bias, proj_weight,
    vit_pre_codes, vit_pre_exps, vit_down, vit_up, vit_mid_codes, vit_mid_exps, mid_gain,
    layer_scale,
):
    f32, b16 = jnp.float32, jnp.bfloat16
    features, width = proj_weight.shape
    units, d_vit = vit_down.shape
    vmem = pl.BlockSpec(memory_space=pltpu.VMEM)
    hbm = pl.BlockSpec(memory_space=pl.ANY)
    scratch = [
        ((features, width), b16), ((units, d_vit), b16), ((units, d_vit), b16),
        ((16, 2, width), b16), ((16, 2, features), b16), ((16, 8, d_vit), b16),
        ((16, 8, d_vit), b16), ((2, 4, 4, 8, d_vit), b16), ((2, 2, 4, 8, d_vit), b16),
        ((2, 4, 8, d_vit), b16), ((2, 3, 8, d_vit), b16), ((2, 4, 8, d_vit), b16),
        ((2, 3, 8, d_vit), b16), ((4, 8, d_vit), f32),
        ((32, features), f32), ((128, d_vit), f32), ((32, width), f32),
        ((units, 128), f32), ((units, 128), f32), ((8, d_vit), f32), ((1, features), f32),
        ((1, features), f32), ((1, d_vit), f32), ((1, d_vit), f32), ((32, 128), f32),
        ((4, 8, 128), f32),
    ]
    outs = [(32, features), (32, width), (units, 128), (128, d_vit), (units, 128), (128, d_vit), (8, d_vit)]
    held = pl.pallas_call(
        fused_kernel,
        out_shape=[jax.ShapeDtypeStruct(shape, b16) for shape in outs],
        in_specs=[vmem] * 14 + [hbm] * 3,
        out_specs=[vmem] * len(outs),
        scratch_shapes=[pltpu.VMEM(s, t) for s, t in scratch]
        + [
            pltpu.SemaphoreType.DMA((6,)), pltpu.SemaphoreType.DMA((80,)),
            pltpu.SemaphoreType.DMA((80,)),
        ],
        compiler_params=pltpu.CompilerParams(
            collective_id=0, has_side_effects=True, vmem_limit_bytes=58 * 2**20
        ),
        cost_estimate=pl.CostEstimate(
            flops=2 * 10**9, bytes_accessed=24 * 10**6, transcendentals=2 * 10**5
        ),
    )(
        grad_dec, token_order.reshape(1, -1), proj_pre_codes, proj_pre_exps,
        projector_norm_input_codes, projector_norm_input_exponents,
        projector_norm_gain.reshape(-1, BLOCK), projector_norm_bias.reshape(-1, BLOCK),
        vit_pre_codes.T, vit_pre_exps, vit_mid_codes, vit_mid_exps,
        mid_gain.reshape(-1, BLOCK), layer_scale.reshape(-1, BLOCK), proj_weight, vit_down,
        vit_up.T,
    )
    steps = 25
    whole = lambda i: (0, 0)
    fifth = lambda i: (0, i // 5)
    gpw, gvd, gvu, gvin = pl.pallas_call(
        weights_kernel,
        grid=(steps,),
        in_specs=[
            pl.BlockSpec((32, features // steps), lambda i: (0, i)),
            pl.BlockSpec((32, width), whole),
            pl.BlockSpec((units, 128), whole),
            pl.BlockSpec((128, FT), fifth),
            pl.BlockSpec((units, 128), whole),
            pl.BlockSpec((128, FT), fifth),
            pl.BlockSpec((8, d_vit), whole),
        ],
        out_specs=[
            pl.BlockSpec((features // steps, width), lambda i: (i, 0)),
            pl.BlockSpec((units, FT), fifth),
            pl.BlockSpec((units, FT), fifth),
            pl.BlockSpec((8, d_vit), whole),
        ],
        out_shape=[
            jax.ShapeDtypeStruct((features, width), b16),
            jax.ShapeDtypeStruct((units, d_vit), b16),
            jax.ShapeDtypeStruct((units, d_vit), b16),
            jax.ShapeDtypeStruct((8, d_vit), b16),
        ],
        compiler_params=pltpu.CompilerParams(vmem_limit_bytes=24 * 2**20),
    )(*held)
    return gpw, gvd, gvu.T, gvin


def solution(mesh):
    fused = mesh.shape["dtp"] == 16
    return jax.shard_map(
        fused_body if fused else body,
        mesh=mesh,
        in_specs=(
            P(("groups", "dtp"), None),
            P("groups"),
            P("groups", "dtp"),
            P("groups", "dtp"),
            P(("groups", "dtp"), None),
            P(("groups", "dtp"), None),
            P(),
            P(),
            P(None, "dtp"),
            P("groups", "dtp"),
            P("groups", "dtp"),
            P("dtp", None),
            P(None, "dtp"),
            P(("groups", "dtp"), None),
            P(("groups", "dtp"), None),
            P(),
            P(),
        ),
        out_specs=(
            P(None, ("groups", "dtp")),
            P("dtp", "groups"),
            P(None, ("groups", "dtp")),
            P(("groups", "dtp"), None),
        ),
        check_vma=False,
    )
```

```python
import math

import jax
import jax.numpy as jnp
from jax import lax
from jax.experimental import pallas as pl
from jax.experimental.pallas import tpu as pltpu
from jax.sharding import PartitionSpec as P


def decode_block_columns(codes, exps):
    rows, cols = codes.shape
    groups = exps.shape[1]
    scale = jnp.exp2((exps - 8).astype(jnp.float32))
    return (
        codes.astype(jnp.float32).reshape(rows, groups, cols // groups) * scale[:, :, None]
    ).reshape(rows, cols)


def dequant_rows(codes, exps):
    rows, cols = codes.shape
    groups = exps.shape[0]
    scale = jnp.exp2((exps - 8).astype(jnp.float32))
    return (
        codes.astype(jnp.float32).reshape(groups, rows // groups, cols) * scale[:, None, :]
    ).reshape(rows, cols)


def gelu_grad(value):
    return 0.5 * (1.0 + jax.scipy.special.erf(value / math.sqrt(2.0))) + value * jnp.exp(
        -0.5 * value * value
    ) / math.sqrt(2.0 * math.pi)


def layer_norm_statistics(merged):
    center = merged - jnp.mean(merged, axis=-1, keepdims=True)
    inverse_deviation = lax.rsqrt(jnp.mean(center * center, axis=-1, keepdims=True) + 1e-05)
    return (center * inverse_deviation, inverse_deviation)


def layer_norm_backward(gradient_input, centered_unit_input, inverse_deviation, norm_gain_vector):
    gain_scaled_gradient = gradient_input * norm_gain_vector
    leading_moment = jnp.mean(gain_scaled_gradient, axis=-1, keepdims=True)
    trailing_moment = jnp.mean(gain_scaled_gradient * centered_unit_input, axis=-1, keepdims=True)
    return inverse_deviation * (
        gain_scaled_gradient - leading_moment - centered_unit_input * trailing_moment
    )


def rms_stats(mid):
    recip = lax.rsqrt(jnp.mean(mid * mid, axis=-1, keepdims=True) + 1e-06)
    return (mid * recip, recip)


def rms_back(gradient_input, uhat, recip, norm_gain_vector):
    gain_scaled_gradient = gradient_input * norm_gain_vector
    return recip * (
        gain_scaled_gradient - uhat * jnp.mean(gain_scaled_gradient * uhat, axis=-1, keepdims=True)
    )


def contract_rows(left, right):
    return lax.dot_general(
        left, right, (((0,), (0,)), ((), ())), preferred_element_type=jnp.float32
    )


def contract_cols(left, right):
    return lax.dot_general(
        left, right, (((1,), (1,)), ((), ())), preferred_element_type=jnp.float32
    )


def body(
    grad_dec,
    token_order,
    proj_pre_codes,
    proj_pre_exps,
    projector_norm_input_codes,
    projector_norm_input_exponents,
    projector_norm_gain,
    projector_norm_bias,
    proj_weight,
    vit_pre_codes,
    vit_pre_exps,
    vit_down,
    vit_up,
    vit_mid_codes,
    vit_mid_exps,
    mid_gain,
    layer_scale,
):
    f32 = jnp.float32
    brain_float_half = jnp.bfloat16
    own_vit = vit_mid_codes.shape[0]
    d_vit = vit_mid_codes.shape[1]
    uhat, recip = rms_stats(decode_block_columns(vit_mid_codes, vit_mid_exps))
    mid_normed = (uhat * mid_gain).astype(brain_float_half)
    received = lax.all_to_all(grad_dec, "dtp", split_axis=1, concat_axis=0, tiled=True)
    inverse = jnp.argsort(token_order)
    grad_act = jnp.take(received, inverse, axis=0)
    proj_pre = decode_block_columns(proj_pre_codes, proj_pre_exps)
    grad_pre = (grad_act.astype(f32) * gelu_grad(proj_pre)).astype(brain_float_half)
    pre = dequant_rows(vit_pre_codes, vit_pre_exps)
    hidden = jax.nn.gelu(pre, approximate=False).astype(brain_float_half)
    vit_rows_all = hidden.shape[0]
    merged_token_codes, merged_token_exponents = (
        lax.all_gather(projector_norm_input_codes, "dtp", axis=0, tiled=True),
        lax.all_gather(projector_norm_input_exponents, "dtp", axis=0, tiled=True),
    )
    centered_unit_input, inverse_deviation = layer_norm_statistics(
        decode_block_columns(merged_token_codes, merged_token_exponents)
    )
    normalized_rows = (centered_unit_input * projector_norm_gain + projector_norm_bias).astype(
        brain_float_half
    )
    grad_proj_weight = contract_rows(normalized_rows, grad_pre).astype(brain_float_half)
    normalized_gradient = contract_cols(grad_pre, proj_weight)
    merged_gradient_term = layer_norm_backward(
        normalized_gradient, centered_unit_input, inverse_deviation, projector_norm_gain
    )
    merged_token_gradient = lax.psum(merged_gradient_term, "dtp").astype(brain_float_half)
    grad_out_all = merged_token_gradient.reshape(vit_rows_all, d_vit)
    grad_out = lax.dynamic_slice_in_dim(grad_out_all, lax.axis_index("dtp") * own_vit, own_vit, 0)
    branch = (grad_out_all.astype(f32) * layer_scale).astype(brain_float_half)
    down_total = contract_rows(hidden, branch)
    grad_hidden = contract_cols(branch, vit_down)
    down_total, grad_hidden = (down_total, grad_hidden)
    grad_vit_down = down_total.astype(brain_float_half)
    grad_vit_pre = (grad_hidden * gelu_grad(pre)).astype(brain_float_half)
    rows = grad_vit_pre
    grad_vit_up = contract_rows(lax.all_gather(mid_normed, "dtp", axis=0, tiled=True), rows).astype(
        brain_float_half
    )
    rows = grad_vit_pre
    grad_mid_normed = lax.psum_scatter(
        contract_cols(rows, vit_up), "dtp", scatter_dimension=0, tiled=True
    )
    grad_vit_in = (grad_out.astype(f32) + rms_back(grad_mid_normed, uhat, recip, mid_gain)).astype(
        brain_float_half
    )
    return (grad_proj_weight, grad_vit_down, grad_vit_up, grad_vit_in)


FT = 640
BLOCK = 128


def fused_kernel(
    gdec, tok, ppc, ppe, mlc, mle, gain2, bias2, pre_c, pre_e, midc, mide, mgain2, lscale2,
    w_h, vd_h, vu_h,
    normed, gp, gvd_h, gvu_h, gvin,
    wv, vdv, vuv, recv, mall, midall, goall, part, rc, ry, rz, sy, sz, acc, scr, nat,
    gact, gg_t, pre_t, mid, gain, bias, mgain, lscale, rsd, stat, hid_t, br, gvp_t,
    lsem, ss, rsem,
):
    f32, b16 = jnp.float32, jnp.bfloat16
    d = lax.axis_index("dtp")
    z, y, c = d // 4, (d // 2) % 2, d % 2
    q_own = 2 * y + c
    core_peer, y_peer = d + 1 - 2 * c, d + 2 - 4 * y
    width = gp.shape[1]
    qw = nat.shape[1]
    tiles = qw // FT
    features = scr.shape[1]
    counter = [0]
    sent = []

    def sem_ids(n):
        counter[0] += n
        return counter[0] - n

    def copy(src, dst, i, peer):
        return pltpu.make_async_remote_copy(
            src_ref=src, dst_ref=dst, send_sem=ss.at[i], recv_sem=rsem.at[i],
            device_id={"dtp": peer}, device_id_type=pl.DeviceIdType.MESH,
        )

    def send(src, dst, i, peer):
        one = copy(src, dst, i, peer)
        one.start()
        sent.append(one)

    def lanes(t, base=0, size=FT):
        return pl.ds(pl.multiple_of(base + t * size, 128), size)

    order = [1 - c, 3 - c, 2 * (1 - y) + c, q_own]
    w_in = []
    for i, q in enumerate(order):
        rows = pl.ds(pl.multiple_of(q * qw, 128), qw)
        one = pltpu.make_async_copy(w_h.at[rows, :], wv.at[rows, :], lsem.at[i])
        one.start()
        w_in.append(one)
    vd_in = pltpu.make_async_copy(vd_h, vdv, lsem.at[4])
    vu_in = pltpu.make_async_copy(vu_h, vuv, lsem.at[5])

    barrier = pltpu.get_barrier_semaphore()
    for k in range(1, 16):
        pl.semaphore_signal(
            barrier, inc=1, device_id={"dtp": (d + k) % 16},
            device_id_type=pl.DeviceIdType.MESH,
        )
    pl.semaphore_wait(barrier, 15)

    class Gather:
        def __init__(self, buf):
            self.buf, self.base = buf, sem_ids(16)

        def go(self, owner, i, peer):
            send(self.buf.at[owner], self.buf.at[owner], self.base + i, peer)

        def arrive(self, owner, i):
            copy(self.buf.at[owner], self.buf.at[owner], self.base + i, core_peer).wait_recv()

        def start(self):
            for k in (1, 2, 3):
                self.go(d, k - 1, (z + k) % 4 * 4 + q_own)
            self.go(d, 3, y_peer)
            self.go(d, 7, core_peer)

        def forward_z(self):
            for k in (1, 3, 2):
                owner = (z + 4 - k) % 4 * 4 + q_own
                self.arrive(owner, k - 1)
                self.go(owner, 3 + k, y_peer)
                self.go(owner, 7 + k, core_peer)

        def forward_y(self):
            for k in (0, 1, 3, 2):
                owner = (z + 4 - k) % 4 * 4 + 2 * (1 - y) + c
                self.arrive(owner, 3 + k)
                self.go(owner, 11 + k, core_peer)

        def finish(self):
            for k in range(4):
                self.arrive((z + 4 - k) % 4 * 4 + 2 * y + 1 - c, 7 + k)
            for k in range(4):
                self.arrive((z + 4 - k) % 4 * 4 + 2 * (1 - y) + 1 - c, 11 + k)

    class Scatter:
        def __init__(self, r):
            self.r, self.base = r, sem_ids(6)

        def core(self, yy):
            send(part.at[self.r, 2 * yy + 1 - c], rc.at[self.r, yy], self.base + yy, core_peer)

        def core_wait(self, yy, i):
            copy(part.at[self.r, 2 * yy + 1 - c], rc.at[self.r, yy], self.base + i, core_peer).wait_recv()

        def middle(self):
            r = self.r

            @pl.loop(0, tiles)
            def _(t):
                s = lanes(t)
                sy[r, :, :, s] = (
                    part[r, 2 * (1 - y) + c, :, :, s].astype(f32)
                    + rc[r, 1 - y, :, :, s].astype(f32)
                ).astype(b16)

            send(sy.at[r], ry.at[r], self.base + 2, y_peer)

        def last(self):
            r = self.r
            copy(sy.at[r], ry.at[r], self.base + 2, y_peer).wait_recv()

            @pl.loop(0, tiles)
            def _(t):
                s = lanes(t)
                acc[:, :, s] = (
                    part[r, q_own, :, :, s].astype(f32) + rc[r, y, :, :, s].astype(f32)
                    + ry[r, :, :, s].astype(f32)
                )

            for k in (2, 1, 3):
                sz[r, k - 1] = acc[(z + k) % 4].astype(b16)
                send(sz.at[r, k - 1], rz.at[r, k - 1], self.base + 2 + k, (z + k) % 4 * 4 + q_own)

        def finish(self):
            r = self.r
            for k in (1, 2, 3):
                copy(sz.at[r, k - 1], rz.at[r, k - 1], self.base + 2 + k, core_peer).wait_recv()
            return (
                acc[z] + rz[r, 0].astype(f32) + rz[r, 1].astype(f32) + rz[r, 2].astype(f32)
            )

    a2a = sem_ids(16)

    def own_columns(p):
        return pl.ds(pl.multiple_of(p * width, 128), width)

    for k in range(1, 16):
        p = (d + k) % 16
        send(gdec.at[:, own_columns(p)], recv.at[d], a2a + k, p)
    mscale = jnp.exp2((mle[...] - 8).astype(f32))
    for j in range(features // BLOCK):
        s = pl.ds(j * BLOCK, BLOCK)
        mall[d, :, s] = (mlc[:, s].astype(f32) * mscale[:, j : j + 1]).astype(b16)
    g_in = Gather(mall)
    g_in.start()
    recv[d] = gdec[:, own_columns(d)]
    pscale = jnp.exp2((ppe[...] - 8).astype(f32))
    proj_grad = jnp.concatenate(
        [
            gelu_grad(ppc[:, BLOCK * j : BLOCK * (j + 1)].astype(f32) * pscale[:, j : j + 1])
            for j in range(width // BLOCK)
        ],
        axis=1,
    )
    for k in range(1, 16):
        p = (d + 16 - k) % 16
        copy(recv.at[p], recv.at[p], a2a + k, p).wait_recv()
    for i in range(16):
        gact[2 * i : 2 * i + 2, :] = recv[i].astype(f32)
    place = (lax.broadcasted_iota(jnp.int32, (32, 32), 0) == tok[...]).astype(f32).astype(b16)
    grad_act = jnp.dot(place, gact[...].astype(b16), preferred_element_type=f32)
    gp[...] = (grad_act * proj_grad).astype(b16)

    s1 = Scatter(0)

    def project(i):
        q = order[i]
        w_in[i].wait()

        @pl.loop(0, tiles)
        def _(t):
            res = contract_cols(gp[...], wv[lanes(t, q * qw), :])
            part[0, q, :, :, lanes(t)] = res.reshape(4, 8, FT).astype(b16)

    project(0)
    s1.core(0)
    g_in.forward_z()
    project(1)
    s1.core(1)
    vd_in.start()
    project(2)
    vu_in.start()
    project(3)
    g_in.forward_y()
    s1.core_wait(0, 0)
    s1.core_wait(1, 1)
    s1.middle()

    for flat, line in ((gain2, gain), (bias2, bias), (mgain2, mgain), (lscale2, lscale)):
        for j in range(flat.shape[0]):
            line[:, BLOCK * j : BLOCK * (j + 1)] = flat[j : j + 1, :]
    dscale = jnp.exp2((mide[...] - 8).astype(f32))
    for j in range(qw // BLOCK):
        s = pl.ds(j * BLOCK, BLOCK)
        mid[:, s] = midc[:, s].astype(f32) * dscale[:, j : j + 1]

    def rms(t):
        s = lanes(t)
        v = mid[:, s]
        return jnp.sum(v * v, axis=-1, keepdims=True)

    rms_sum = lax.fori_loop(0, tiles, lambda t, a: a + rms(t), jnp.zeros((8, 1), f32))
    recip = lax.rsqrt(rms_sum / qw + 1e-06)

    @pl.loop(0, tiles)
    def _(t):
        s = lanes(t)
        midall[d, :, s] = (mid[:, s] * recip * mgain[:, s]).astype(b16)

    s1.last()
    g_mid = Gather(midall)

    g_in.finish()
    all_tiles = features // FT
    zero = jnp.zeros((32, 1), f32)

    def mean_step(t, a):
        s = lanes(t)
        for i in range(16):
            scr[2 * i : 2 * i + 2, s] = mall[i, :, s].astype(f32)
        return a + jnp.sum(scr[:, s], axis=-1, keepdims=True)

    mean = lax.fori_loop(0, all_tiles, mean_step, zero) / features

    def var_step(t, a):
        s = lanes(t)
        center = scr[:, s] - mean
        scr[:, s] = center
        return a + jnp.sum(center * center, axis=-1, keepdims=True)

    variance = lax.fori_loop(0, all_tiles, var_step, zero) / features
    rsd[...] = jnp.broadcast_to(lax.rsqrt(variance + 1e-05), rsd.shape)

    total = s1.finish()
    own_rows = pl.ds(pl.multiple_of(z * 8, 8), 8)
    own_lanes = pl.ds(pl.multiple_of(q_own * qw, 128), qw)
    rstd8 = rsd[own_rows, 0:1]
    gy = total * gain[:, own_lanes]
    xh = scr[own_rows, own_lanes] * rstd8
    first = jnp.sum(gy, axis=-1, keepdims=True)
    second = jnp.sum(gy * xh, axis=-1, keepdims=True)
    lane = lax.broadcasted_iota(jnp.int32, (8, 128), 1)
    stat[0] = jnp.where(lane < 64, first, second)
    st = sem_ids(3)
    plane = [core_peer, y_peer, 4 * z + 3 - q_own]
    for j in range(3):
        send(stat.at[0], stat.at[j + 1], st + j, plane[j])
    for j in range(3):
        copy(stat.at[0], stat.at[j + 1], st + j, plane[j]).wait_recv()
    sums = (stat[0] + stat[1] + stat[2] + stat[3]) / features
    lead, trail = sums[:, 0:1], sums[:, 64:65]
    goall[d] = (rstd8 * (gy - lead - xh * trail)).astype(b16)
    g_out = Gather(goall)
    g_out.start()

    @pl.loop(0, all_tiles)
    def _(t):
        s = lanes(t)
        normed[:, s] = (scr[:, s] * rsd[:, 0:1] * gain[:, s] + bias[:, s]).astype(b16)

    g_out.forward_z()
    g_mid.start()
    spread = jnp.broadcast_to(jnp.exp2((pre_e[...] - 8).astype(f32)) / 16, (16, vdv.shape[0]))
    pre_t[...] = contract_rows(spread.astype(b16), jnp.ones((16, 128), b16))
    units = 160

    @pl.loop(0, vdv.shape[0] // units)
    def _(t):
        s = pl.ds(pl.multiple_of(t * units, 32), units)
        v = pre_c[s, :].astype(f32) * pre_t[s, :]
        cdf = 0.5 * (1.0 + lax.erf(v / math.sqrt(2.0)))
        hid_t[s, :] = (v * cdf).astype(b16)
        gg_t[s, :] = cdf + v * jnp.exp(-0.5 * v * v) / math.sqrt(2.0 * math.pi)

    g_out.forward_y()
    g_out.finish()
    g_mid.forward_z()

    vrow = lax.broadcasted_iota(jnp.int32, (128, 128), 0)
    held = lax.broadcasted_iota(jnp.int32, (128, 128), 1)
    vision = held // 32 * 32 + held % 8 * 4 + held // 8 % 4
    shuffle = (vrow == vision).astype(f32).astype(b16)

    @pl.loop(0, tiles)
    def _(t):
        s = lanes(t)
        block = goall[:, :, s].astype(f32).reshape(128, FT).astype(b16)
        rows = jnp.dot(shuffle, block, preferred_element_type=f32)
        nat[:, s] = rows
        br[:, s] = (rows * lscale[:, s]).astype(b16)

    vd_in.wait()

    @pl.loop(0, vdv.shape[0] // units)
    def _(t):
        s = pl.ds(pl.multiple_of(t * units, 32), units)
        gvp_t[s, :] = (contract_cols(vdv[s, :], br[...]) * gg_t[s, :]).astype(b16)

    vu_in.wait()

    @pl.loop(0, tiles)
    def _(t):
        s = lanes(t)
        res = contract_rows(gvp_t[...], vuv[:, s]).reshape(4, 4, 8, FT)
        for q in range(4):
            part[1, q, :, :, s] = res[:, q].astype(b16)

    s2 = Scatter(1)
    s2.core(0)
    s2.core(1)
    g_mid.forward_y()

    def down_grad(first, count):
        @pl.loop(first, first + count)
        def _(t):
            s = pl.ds(pl.multiple_of(t * units, 32), units)
            vdv[s, :] = jnp.dot(hid_t[s, :], br[...], preferred_element_type=f32).astype(b16)

    down_grad(0, 2)
    s2.core_wait(0, 0)
    s2.core_wait(1, 1)
    s2.middle()

    down_grad(2, 3)
    vd_out = pltpu.make_async_copy(vdv, gvd_h, lsem.at[4])
    vd_out.start()
    s2.last()
    g_mid.finish()

    @pl.loop(0, tiles)
    def _(t):
        s = lanes(t)
        block = midall[:, :, s].astype(f32).reshape(128, FT).astype(b16)
        vuv[:, s] = jnp.dot(gvp_t[...], block, preferred_element_type=f32).astype(b16)

    vu_out = pltpu.make_async_copy(vuv, gvu_h, lsem.at[5])
    vu_out.start()
    gn = s2.finish() * mgain[...]
    uhat = mid[...] * recip
    back = recip * (gn - uhat * jnp.mean(gn * uhat, axis=-1, keepdims=True))
    gvin[...] = (nat[pl.ds(pl.multiple_of(d * 8, 8), 8), :] + back).astype(b16)
    for one in sent:
        one.wait_send()
    vd_out.wait()
    vu_out.wait()


def weights_kernel(normed, gp, gvd_in, gvu_in, gvin, gpw, gvd, gvu, out):
    gpw[...] = contract_rows(normed[...], gp[...]).astype(jnp.bfloat16)
    gvd[...] = gvd_in[...]
    gvu[...] = gvu_in[...]

    @pl.when(pl.program_id(0) == 0)
    def _():
        out[...] = gvin[...]


def fused_body(
    grad_dec, token_order, proj_pre_codes, proj_pre_exps, projector_norm_input_codes,
    projector_norm_input_exponents, projector_norm_gain, projector_norm_bias, proj_weight,
    vit_pre_codes, vit_pre_exps, vit_down, vit_up, vit_mid_codes, vit_mid_exps, mid_gain,
    layer_scale,
):
    f32, b16 = jnp.float32, jnp.bfloat16
    features, width = proj_weight.shape
    units, d_vit = vit_down.shape
    vmem = pl.BlockSpec(memory_space=pltpu.VMEM)
    hbm = pl.BlockSpec(memory_space=pl.ANY)
    scratch = [
        ((features, width), b16), ((units, d_vit), b16), ((units, d_vit), b16),
        ((16, 2, width), b16), ((16, 2, features), b16), ((16, 8, d_vit), b16),
        ((16, 8, d_vit), b16), ((2, 4, 4, 8, d_vit), b16), ((2, 2, 4, 8, d_vit), b16),
        ((2, 4, 8, d_vit), b16), ((2, 3, 8, d_vit), b16), ((2, 4, 8, d_vit), b16),
        ((2, 3, 8, d_vit), b16), ((4, 8, d_vit), f32),
        ((32, features), f32), ((128, d_vit), f32), ((32, width), f32),
        ((units, 128), f32), ((units, 128), f32), ((8, d_vit), f32), ((1, features), f32),
        ((1, features), f32), ((1, d_vit), f32), ((1, d_vit), f32), ((32, 128), f32),
        ((4, 8, 128), f32), ((units, 128), b16), ((128, d_vit), b16), ((units, 128), b16),
    ]
    outs = [(32, features), (32, width), (units, d_vit), (units, d_vit), (8, d_vit)]
    held = pl.pallas_call(
        fused_kernel,
        out_shape=[jax.ShapeDtypeStruct(shape, b16) for shape in outs],
        in_specs=[vmem] * 14 + [hbm] * 3,
        out_specs=[vmem, vmem, hbm, hbm, vmem],
        scratch_shapes=[pltpu.VMEM(s, t) for s, t in scratch]
        + [
            pltpu.SemaphoreType.DMA((6,)), pltpu.SemaphoreType.DMA((80,)),
            pltpu.SemaphoreType.DMA((80,)),
        ],
        compiler_params=pltpu.CompilerParams(
            collective_id=0, has_side_effects=True, vmem_limit_bytes=58 * 2**20
        ),
        cost_estimate=pl.CostEstimate(
            flops=2 * 10**9, bytes_accessed=24 * 10**6, transcendentals=2 * 10**5
        ),
    )(
        grad_dec, token_order.reshape(1, -1), proj_pre_codes, proj_pre_exps,
        projector_norm_input_codes, projector_norm_input_exponents,
        projector_norm_gain.reshape(-1, BLOCK), projector_norm_bias.reshape(-1, BLOCK),
        vit_pre_codes.T, vit_pre_exps, vit_mid_codes, vit_mid_exps,
        mid_gain.reshape(-1, BLOCK), layer_scale.reshape(-1, BLOCK), proj_weight, vit_down,
        vit_up.T,
    )
    steps = 25
    whole = lambda i: (0, 0)
    vit_rows = pl.BlockSpec((units // steps, d_vit), lambda i: (i, 0))
    gpw, gvd, gvu, gvin = pl.pallas_call(
        weights_kernel,
        grid=(steps,),
        in_specs=[
            pl.BlockSpec((32, features // steps), lambda i: (0, i)),
            pl.BlockSpec((32, width), whole),
            vit_rows,
            vit_rows,
            pl.BlockSpec((8, d_vit), whole),
        ],
        out_specs=[
            pl.BlockSpec((features // steps, width), lambda i: (i, 0)),
            vit_rows,
            vit_rows,
            pl.BlockSpec((8, d_vit), whole),
        ],
        out_shape=[
            jax.ShapeDtypeStruct((features, width), b16),
            jax.ShapeDtypeStruct((units, d_vit), b16),
            jax.ShapeDtypeStruct((units, d_vit), b16),
            jax.ShapeDtypeStruct((8, d_vit), b16),
        ],
        compiler_params=pltpu.CompilerParams(vmem_limit_bytes=60 * 2**20),
    )(*held)
    return gpw, gvd, gvu.T, gvin


def solution(mesh):
    fused = mesh.shape["dtp"] == 16
    return jax.shard_map(
        fused_body if fused else body,
        mesh=mesh,
        in_specs=(
            P(("groups", "dtp"), None),
            P("groups"),
            P("groups", "dtp"),
            P("groups", "dtp"),
            P(("groups", "dtp"), None),
            P(("groups", "dtp"), None),
            P(),
            P(),
            P(None, "dtp"),
            P("groups", "dtp"),
            P("groups", "dtp"),
            P("dtp", None),
            P(None, "dtp"),
            P(("groups", "dtp"), None),
            P(("groups", "dtp"), None),
            P(),
            P(),
        ),
        out_specs=(
            P(None, ("groups", "dtp")),
            P("dtp", "groups"),
            P(None, ("groups", "dtp")),
            P(("groups", "dtp"), None),
        ),
        check_vma=False,
    )
```
